32 devices in a mesh: engine: 4 (over x, core), expert: 8 (over z, y).
Axes of the slice: x: 2, y: 2, z: 4, core: 2. Of those that a mesh axis runs over, the one named last changes fastest.
Arguments:
- tokens: bfloat16 [2, 4096, 4096], P(None, ('engine', 'expert')), may hold values from -6 to 6
- expert_ids: int32 [2, 4096, 2], P(None, ('engine', 'expert')), may hold values from 0 to 7, all different within a row; in each aligned block of 128 rows (0 to 127, 128 to 255, ..., all dimensions but the last counted through in order) at most 48 rows name the same one
- route_gain: float32 [2, 4096, 2], P(None, ('engine', 'expert')), may hold values from 0.1 to 1
- gate_up_master: float32 [8, 4096, 1536], P('expert', 'engine'), may hold values from -0.09375 to 0.09375
- gate_up_moment: float32 [8, 4096, 1536], P('expert', 'engine'), may hold values from -0.09375 to 0.09375
- gate_up_grad: bfloat16 [8, 4096, 1536], P('expert', 'engine'), may hold values from -0.09375 to 0.09375
- down_master: float32 [8, 768, 4096], P('expert', None, 'engine'), may hold values from -0.21875 to 0.21875
- down_moment: float32 [8, 768, 4096], P('expert', None, 'engine'), may hold values from -0.21875 to 0.21875
- down_grad: bfloat16 [8, 768, 4096], P('expert', None, 'engine'), may hold values from -0.21875 to 0.21875
Outputs:
- mixed: bfloat16 [2, 4096, 4096], P(None, ('engine', 'expert'))
The draws below stay inside these ranges and needn't reach their ends.
Inputs may be any that keep to these rules, and one draw needn't show every extreme that they name: `expert_ids`: in each aligned block of 128 rows of one step, no expert is named by more than 48 rows, a bound that some block reaches; a row names 2 different experts.
All inputs are finite; a program needn't handle non-finite values.
Results may differ from the reference program's by a relative error of at most 0.0081.
Values may be sent and summed in bfloat16 or wider, within the bound.
A program may use at most 128 MiB of HBM per device.

```python
import math
import jax
import jax.numpy as jnp
import numpy as np
from jax import lax

D = 4096
FF = 768
TOP = 2
STEPS = 2
ROW_DEV = 128
EXPERTS = 8
CAP = 48
ROWS = 4096
N_ENGINE = 4
N_EXPERT = 8


def level_of(key, dims, shards, least, largest):
    factor_of, own = 1.0, jax.random.fold_in(key, 6)
    for dim, parts in shards:
        heights = jnp.exp(jax.random.uniform(jax.random.fold_in(own, dim), (parts,), jnp.float32, least / len(shards), largest / len(shards)))
        factor_of = factor_of * jnp.repeat(heights, dims[dim] // parts).reshape([-1 if axis == dim else 1 for axis in range(len(dims))])
    return factor_of


def deal_out(rng, own, number, rows, amount, top, bound, lean):
    order = jax.random.permutation(rng, amount)
    heavy_load, common = portions_of(amount, rows * top, bound, lean, True), portions_of(amount, rows * top, bound, lean, False)
    places = jnp.arange(amount)

    def named(tallies, offset_by):
        used = int((tallies > 0).sum())
        fixed = max(1, used // 4)
        shifted = fixed + (places - fixed + offset_by * (used - fixed)) % max(1, amount - fixed)
        return jnp.zeros((amount,), jnp.int32).at[order[jnp.where(places < fixed, places, shifted)]].set(jnp.asarray(tallies, jnp.int32))

    tallies = jnp.where(number % 4 == 0, named(heavy_load, number // 4), named(common, number - number // 4 - 1))
    mixed = jax.random.permutation(jax.random.fold_in(own, 3), amount)
    donor, sink = mixed[0:amount // 2 * 2:2], mixed[1:amount // 2 * 2:2]
    margin = jnp.minimum(tallies[donor] - 1, bound - tallies[sink]) // 2
    margin = jnp.where((donor == order[0]) | (sink == order[0]) | (tallies[sink] == 0), 0, jnp.maximum(margin, 0))
    shifted = jax.random.randint(jax.random.fold_in(own, 4), (amount // 2,), 0, 1 << 20) % (margin + 1)
    tallies = tallies.at[donor].add(-shifted).at[sink].add(shifted)
    items = jnp.searchsorted(jnp.cumsum(tallies), jnp.arange(rows * top), side="right").astype(jnp.int32)
    grid = items.reshape(top, rows).T
    grid = grid[jax.random.permutation(jax.random.fold_in(own, 1), rows)]
    offset_by = jax.random.randint(jax.random.fold_in(own, 2), (rows, 1), 0, top)
    return jnp.take_along_axis(grid, (jnp.arange(top)[None, :] + offset_by) % top, axis=1)


def portions_of(amount, total, most, slope, full):
    loads = [(1 << 20) // math.isqrt(grade ** slope) + 1 for grade in range(1, amount + 1)]
    largest = most if full else min(most, max(-(-total // amount), total * loads[0] // sum(loads)))
    least = 1 if total - largest >= amount - 1 else 0
    holding, rest = [largest] + [least] * (amount - 1), total - largest - least * (amount - 1)
    while rest > 0:
        movable = [i for i in range(1, amount) if holding[i] < largest] or [i for i in range(1, amount) if holding[i] < most]
        mass, budget = sum([loads[i] for i in movable]), rest
        for i in movable:
            more = min(most - holding[i], max(1, budget * loads[i] // mass), rest)
            holding[i] = holding[i] + more
            rest = rest - more
    return np.array(holding)


def centred(rng, dims, width, bound, pieces=(), kind=jnp.bfloat16):
    entries = jax.random.normal(rng, dims, jnp.float32) * width
    if len(pieces) > 0:
        entries = level_of(rng, dims, pieces, -0.22, 0.18) * entries
    return jnp.clip(entries, min=-bound, max=bound).astype(kind)


def setup_inputs(seed: int = 0) -> dict:
    key_list = jax.random.split(jax.random.key(seed), 10)
    tokens = centred(key_list[0], (STEPS, ROWS, D), 1.0, 6.0, ((1, 32),))
    expert_ids_keys = jax.random.split(jax.random.fold_in(key_list[1], 1), STEPS * ROWS // ROW_DEV)
    expert_ids_turns = jax.random.permutation(jax.random.fold_in(key_list[1], 3), STEPS * ROWS // ROW_DEV)
    expert_ids = jax.vmap(lambda own, number: deal_out(jax.random.fold_in(key_list[1], 2), own, number, ROW_DEV, EXPERTS, TOP, CAP, 2))(expert_ids_keys, expert_ids_turns).reshape((STEPS, ROWS, TOP))
    route_gain = jnp.clip(jnp.exp(math.log(1.0) - 2.3025851 * jax.random.uniform(key_list[2], (STEPS, ROWS, TOP), jnp.float32) ** level_of(key_list[2], (STEPS, ROWS, TOP), ((1, 32),), -0.2, 0.2)), 0.1, 1.0)
    gate_up_master = centred(key_list[3], (EXPERTS, D, 2 * FF), D ** -0.5, 0.09375, ((0, 8), (1, 4)), jnp.float32)
    gate_up_moment = centred(key_list[4], (EXPERTS, D, 2 * FF), D ** -0.5, 0.09375, ((0, 8), (1, 4)), jnp.float32)
    gate_up_grad = centred(key_list[5], (EXPERTS, D, 2 * FF), D ** -0.5, 0.09375, ((0, 8), (1, 4)))
    down_master = centred(key_list[6], (EXPERTS, FF, D), FF ** -0.5, 0.21875, ((0, 8), (2, 4)), jnp.float32)
    down_moment = centred(key_list[7], (EXPERTS, FF, D), FF ** -0.5, 0.21875, ((0, 8), (2, 4)), jnp.float32)
    down_grad = centred(key_list[8], (EXPERTS, FF, D), FF ** -0.5, 0.21875, ((0, 8), (2, 4)))
    return dict(tokens=tokens, expert_ids=expert_ids, route_gain=route_gain, gate_up_master=gate_up_master, gate_up_moment=gate_up_moment, gate_up_grad=gate_up_grad, down_master=down_master, down_moment=down_moment, down_grad=down_grad)


def updated(master, moment, grad):
    return (master - 0.5 * (0.8 * moment + 0.2 * grad.astype(jnp.float32))).astype(jnp.bfloat16)


def expert_apply(packed):
    rows_e, gate_up, down = packed
    flat = rows_e.reshape(-1, D)
    projected = jnp.dot(flat, gate_up, preferred_element_type=jnp.float32)
    hidden = (jax.nn.silu(projected[:, :FF]) * projected[:, FF:]).astype(jnp.bfloat16)
    result = jnp.dot(hidden, down, preferred_element_type=jnp.float32).astype(jnp.bfloat16)
    return result.reshape(rows_e.shape)


def reference(tokens, expert_ids, route_gain, gate_up_master, gate_up_moment, gate_up_grad, down_master, down_moment, down_grad):
    gate_up_weight = updated(gate_up_master, gate_up_moment, gate_up_grad)
    down_weight = updated(down_master, down_moment, down_grad)
    blocks = N_ENGINE * N_EXPERT
    flat_ids = expert_ids.reshape(STEPS, blocks, ROW_DEV * TOP)
    picked = (flat_ids[..., None] == jnp.arange(EXPERTS, dtype=jnp.int32)).astype(jnp.int32)
    earlier = jnp.cumsum(picked, axis=2) - picked
    slot_index = jnp.sum(earlier * picked, axis=3).astype(jnp.int32)
    target = (flat_ids * CAP + slot_index).reshape(STEPS, blocks, ROW_DEV, TOP).astype(jnp.int32)
    rows = tokens.reshape(STEPS, blocks, ROW_DEV, D)
    step_index = jnp.arange(STEPS, dtype=jnp.int32)[:, None, None]
    block_index = jnp.arange(blocks, dtype=jnp.int32)[None, :, None]
    buffer = jnp.zeros((STEPS, blocks, EXPERTS * CAP, D), jnp.bfloat16)
    for k in range(TOP):
        buffer = buffer.at[step_index, block_index, target[..., k]].set(rows)
    per_expert = jnp.moveaxis(buffer.reshape(STEPS, blocks, EXPERTS, CAP, D), 2, 0)
    outputs = lax.map(expert_apply, (per_expert, gate_up_weight, down_weight))
    outputs = jnp.moveaxis(outputs, 0, 2).reshape(STEPS, blocks, EXPERTS * CAP, D)
    share = (route_gain / jnp.sum(route_gain, axis=2, keepdims=True)).astype(jnp.bfloat16)
    share = share.reshape(STEPS, blocks, ROW_DEV, TOP)
    total = jnp.zeros((STEPS, blocks, ROW_DEV, D), jnp.float32)
    for k in range(TOP):
        picked_rows = outputs[step_index, block_index, target[..., k]].astype(jnp.float32)
        total = total + share[..., k, None].astype(jnp.float32) * picked_rows
    return total.astype(jnp.bfloat16).reshape(STEPS, ROWS, D)
```

```python
import functools

import jax
import jax.numpy as jnp
from jax import lax
from jax.experimental import pallas as pl
from jax.experimental.pallas import tpu as pltpu
from jax.sharding import PartitionSpec as P

MESH = pl.DeviceIdType.MESH
TILE = 512


def updated(master, moment, grad):
    return (master - 0.5 * (0.8 * moment + 0.2 * grad.astype(jnp.float32))).astype(jnp.bfloat16)


def layer_kernel(
    n_engine,
    n_expert,
    cap,
    tokens,
    near_tab,
    far_tab,
    gu_master,
    gu_moment,
    gu_grad,
    dn_master,
    dn_moment,
    dn_grad,
    mixed,
    gate_up,
    down,
    own_rows,
    far_rows,
    relay_tab,
    near_send,
    far_send,
    slots,
    hidden,
    near_back,
    far_back,
    part_send,
    part_recv,
    gu_stage,
    gu_grad_stage,
    dn_stage,
    dn_grad_stage,
    local_sem,
    stage_sem,
    token_send,
    token_recv,
    slot_send,
    slot_recv,
    weight_send,
    weight_recv,
):
    half = n_expert // 2
    pairs = n_engine // 2
    steps, rows, width = own_rows.shape
    places = half * cap
    ff = down.shape[0]
    g, e = lax.axis_index("engine"), lax.axis_index("expert")
    core, pair = lax.rem(g, 2), g // 2
    side, me = e // half, lax.rem(e, half)
    partner = (g, lax.rem(e + half, n_expert))
    sibling = (pair * 2 + 1 - core, e)

    def near(j):
        return lax.rem(me + j, half)

    def near_device(j):
        return (g, side * half + near(j))

    def same_core(q):
        return (lax.rem(pair + q, pairs) * 2 + core, e)

    def seats(index, base=0):
        return pl.ds(pl.multiple_of(base + index * cap, 16), cap)

    sends = []

    def send(src, dst, send_sem, recv_sem, device):
        copy = pltpu.make_async_remote_copy(
            src_ref=src, dst_ref=dst, send_sem=send_sem, recv_sem=recv_sem,
            device_id=device, device_id_type=MESH,
        )
        copy.start()
        sends.append(copy)

    def arrive(dst, send_sem, recv_sem, device):
        pltpu.make_async_remote_copy(
            src_ref=dst, dst_ref=dst, send_sem=send_sem, recv_sem=recv_sem,
            device_id=device, device_id_type=MESH,
        ).wait_recv()

    peers = [partner, sibling]
    peers += [near_device(j) for j in range(1, half)]
    peers += [same_core(q) for q in range(1, pairs)]
    barrier = pltpu.get_barrier_semaphore()
    for device in peers:
        pl.semaphore_signal(barrier, inc=1, device_id=device, device_id_type=MESH)
    pl.semaphore_wait(barrier, len(peers))

    send(far_tab, relay_tab, token_send.at[2 * steps], token_recv.at[2 * steps], partner)
    for s in range(steps):
        send(tokens.at[s], far_rows.at[s], token_send.at[s], token_recv.at[s], partner)
    own_copy = pltpu.make_async_copy(tokens, own_rows, local_sem.at[4 * steps])
    own_copy.start()

    gu_rows, dn_cols = gu_master.shape[1], dn_master.shape[2]
    gu_chunk, dn_chunk = gu_stage.shape[2], dn_stage.shape[2]
    n_gu, n_dn = gu_rows // gu_chunk, ff // dn_chunk
    chunks = n_gu + n_dn

    def weight_part(c, owner):
        if c < n_gu:
            start = pl.multiple_of(owner * gu_rows + c * gu_chunk, 16)
            return gate_up.at[pl.ds(start, gu_chunk)]
        columns = pl.ds(pl.multiple_of(owner * dn_cols, 128), dn_cols)
        return down.at[pl.ds((c - n_gu) * dn_chunk, dn_chunk), columns]

    def staged(c):
        slot = c % 2
        if c < n_gu:
            part = pl.ds(c * gu_chunk, gu_chunk)
            refs = (gu_master, gu_moment, gu_grad)
            stages = (gu_stage.at[slot, 0], gu_stage.at[slot, 1], gu_grad_stage.at[slot])
        else:
            part = pl.ds((c - n_gu) * dn_chunk, dn_chunk)
            refs = (dn_master, dn_moment, dn_grad)
            stages = (dn_stage.at[slot, 0], dn_stage.at[slot, 1], dn_grad_stage.at[slot])
        return [
            pltpu.make_async_copy(ref.at[0, part], stage, stage_sem.at[c, i])
            for i, (ref, stage) in enumerate(zip(refs, stages))
        ]

    for copy in staged(0):
        copy.start()
    for c in range(chunks):
        if c + 1 < chunks:
            for copy in staged(c + 1):
                copy.start()
        for copy in staged(c):
            copy.wait()
        slot = c % 2
        mine = weight_part(c, g)
        if c < n_gu:
            mine[...] = updated(gu_stage[slot, 0], gu_stage[slot, 1], gu_grad_stage[slot])
        else:
            mine[...] = updated(dn_stage[slot, 0], dn_stage[slot, 1], dn_grad_stage[slot])
        for q in range(1, pairs):
            send(mine, mine, weight_send.at[c, q], weight_recv.at[c, q], same_core(q))
        send(mine, mine, weight_send.at[c, 0], weight_recv.at[c, 0], sibling)

    def relay(c):
        for q in range(1, pairs):
            owner = lax.rem(pair - q + pairs, pairs) * 2 + core
            part = weight_part(c, owner)
            arrive(part, weight_send.at[c, q], weight_recv.at[c, q], sibling)
            k = pairs + q - 1
            send(part, part, weight_send.at[c, k], weight_recv.at[c, k], sibling)

    def relayed(c):
        arrive(weight_part(c, g + 1 - 2 * core), weight_send.at[c, 0], weight_recv.at[c, 0], sibling)
        for q in range(1, pairs):
            owner = lax.rem(pair - q + pairs, pairs) * 2 + 1 - core
            k = pairs + q - 1
            arrive(weight_part(c, owner), weight_send.at[c, k], weight_recv.at[c, k], sibling)

    def hand_out(s, kind, table, source, outgoing):
        @pl.loop(0, width // TILE)
        def _(t):
            columns = pl.ds(pl.multiple_of(t * TILE, TILE), TILE)
            outgoing[s, :, columns] = jnp.dot(
                table[s, 0], source[s, :, columns], preferred_element_type=jnp.float32
            ).astype(jnp.bfloat16)

        base = kind * places
        for j in range(1, half):
            send(
                outgoing.at[s, seats(near(j))], slots.at[s, seats(me, base)],
                slot_send.at[kind, s, j], slot_recv.at[kind, s, j], near_device(j),
            )
        keep = pltpu.make_async_copy(
            outgoing.at[s, seats(me)], slots.at[s, seats(me, base)], local_sem.at[kind * steps + s]
        )
        keep.start()
        return keep

    own_copy.wait()
    kept = {}
    for s in range(steps):
        kept[0, s] = hand_out(s, 0, near_tab, own_rows, near_send)
    arrive(relay_tab, token_send.at[2 * steps], token_recv.at[2 * steps], partner)
    for s in range(steps):
        arrive(far_rows.at[s], token_send.at[s], token_recv.at[s], partner)
        kept[1, s] = hand_out(s, 1, relay_tab, far_rows, far_send)
        for c in range(s * n_gu // steps, (s + 1) * n_gu // steps):
            relay(c)
    for c in range(n_gu):
        relayed(c)

    def project(s):
        for kind in range(2):
            kept[kind, s].wait()
            for j in range(1, half):
                origin = lax.rem(me - j + half, half)
                arrive(
                    slots.at[s, seats(origin, kind * places)],
                    slot_send.at[kind, s, j], slot_recv.at[kind, s, j], near_device(j),
                )

        @pl.loop(0, ff // 256)
        def _(t):
            left = pl.ds(pl.multiple_of(t * 256, 256), 256)
            right = pl.ds(pl.multiple_of(ff + t * 256, 256), 256)
            gate = jnp.dot(slots[s], gate_up[:, left], preferred_element_type=jnp.float32)
            up = jnp.dot(slots[s], gate_up[:, right], preferred_element_type=jnp.float32)
            hidden[s, :, left] = (gate / (1.0 + jnp.exp(-gate)) * up).astype(jnp.bfloat16)

    def expand(s):
        @pl.loop(0, width // TILE)
        def _(t):
            columns = pl.ds(pl.multiple_of(t * TILE, TILE), TILE)
            slots[s, :, columns] = jnp.dot(
                hidden[s], down[:, columns], preferred_element_type=jnp.float32
            ).astype(jnp.bfloat16)

        for kind, back in ((1, far_back), (0, near_back)):
            for j in range(1, half):
                send(
                    slots.at[s, seats(near(j), kind * places)], back.at[s, seats(me)],
                    slot_send.at[2 + kind, s, j], slot_recv.at[2 + kind, s, j], near_device(j),
                )
            keep = pltpu.make_async_copy(
                slots.at[s, seats(me, kind * places)], back.at[s, seats(me)],
                local_sem.at[(2 + kind) * steps + s],
            )
            keep.start()
            kept[2 + kind, s] = keep

    def back_here(s, kind, back):
        kept[2 + kind, s].wait()
        for j in range(1, half):
            origin = lax.rem(me - j + half, half)
            arrive(
                back.at[s, seats(origin)],
                slot_send.at[2 + kind, s, j], slot_recv.at[2 + kind, s, j], near_device(j),
            )

    def weighted(table, s, back, columns):
        return lax.dot_general(
            table[s, 1], back[s, :, columns], (((0,), (0,)), ((), ())),
            preferred_element_type=jnp.float32,
        )

    for s in range(steps):
        project(s)
        if s == 0:
            for c in range(n_gu, chunks):
                relay(c)
            for c in range(n_gu, chunks):
                relayed(c)
        expand(s)

    for s in range(steps):
        back_here(s, 1, far_back)

        @pl.loop(0, width // TILE)
        def _(t):
            columns = pl.ds(pl.multiple_of(t * TILE, TILE), TILE)
            part_send[s, :, columns] = weighted(relay_tab, s, far_back, columns).astype(jnp.bfloat16)

        send(
            part_send.at[s], part_recv.at[s],
            token_send.at[steps + s], token_recv.at[steps + s], partner,
        )

    for s in range(steps):
        back_here(s, 0, near_back)
        arrive(part_recv.at[s], token_send.at[steps + s], token_recv.at[steps + s], partner)

        @pl.loop(0, width // TILE)
        def _(t):
            columns = pl.ds(pl.multiple_of(t * TILE, TILE), TILE)
            total = weighted(near_tab, s, near_back, columns)
            total = total + part_recv[s, :, columns].astype(jnp.float32)
            mixed[s, :, columns] = total.astype(jnp.bfloat16)

    for copy in sends:
        copy.wait_send()


def per_device(
    tokens,
    expert_ids,
    route_gain,
    gate_up_master,
    gate_up_moment,
    gate_up_grad,
    down_master,
    down_moment,
    down_grad,
):
    steps, rows, top_k = expert_ids.shape
    width = tokens.shape[2]
    n_engine, n_expert = lax.axis_size("engine"), lax.axis_size("expert")
    half, pairs = n_expert // 2, n_engine // 2
    cap = 3 * rows * top_k // (2 * n_expert)
    cap = -(-cap // 16) * 16
    places = half * cap
    ff = down_master.shape[1]

    named = expert_ids[:, None, :, :] == jnp.arange(n_expert, dtype=jnp.int32)[None, :, None, None]
    share = (route_gain / jnp.sum(route_gain, axis=2, keepdims=True)).astype(jnp.bfloat16)
    chosen = jnp.any(named, axis=3)
    portion = jnp.sum(jnp.where(named, share[:, None].astype(jnp.float32), 0.0), axis=3)
    ahead = jnp.arange(rows)[:, None] < jnp.arange(rows)[None, :]
    place = jnp.einsum(
        "ser,rq->seq", chosen.astype(jnp.bfloat16), ahead.astype(jnp.bfloat16),
        preferred_element_type=jnp.float32,
    ).astype(jnp.int32)
    match = chosen[:, :, None, :] & (
        place[:, :, None, :] == jnp.arange(cap, dtype=jnp.int32)[None, None, :, None]
    )
    table = jnp.stack(
        [match.astype(jnp.bfloat16), jnp.where(match, portion[:, :, None, :], 0.0).astype(jnp.bfloat16)],
        axis=1,
    ).reshape(steps, 2, 2, places, rows)
    side = lax.axis_index("expert") // half
    near_tab = lax.dynamic_index_in_dim(table, side, 2, keepdims=False)
    far_tab = lax.dynamic_index_in_dim(table, 1 - side, 2, keepdims=False)

    gu_rows, dn_cols = gate_up_master.shape[1], down_master.shape[2]
    gu_chunk, dn_chunk = min(128, gu_rows), ff // 4
    chunks = gu_rows // gu_chunk + 4
    bf16, f32 = jnp.bfloat16, jnp.float32
    dma = pltpu.SemaphoreType.DMA
    hbm, vmem = pl.BlockSpec(memory_space=pl.ANY), pl.BlockSpec(memory_space=pltpu.VMEM)
    return pl.pallas_call(
        functools.partial(layer_kernel, n_engine, n_expert, cap),
        out_shape=jax.ShapeDtypeStruct(tokens.shape, bf16),
        in_specs=[hbm, vmem, vmem] + [hbm] * 6,
        out_specs=vmem,
        scratch_shapes=[
            pltpu.VMEM((width, 2 * ff), bf16),
            pltpu.VMEM((ff, width), bf16),
            pltpu.VMEM((steps, rows, width), bf16),
            pltpu.VMEM((steps, rows, width), bf16),
            pltpu.VMEM((steps, 2, places, rows), bf16),
            pltpu.VMEM((steps, places, width), bf16),
            pltpu.VMEM((steps, places, width), bf16),
            pltpu.VMEM((steps, 2 * places, width), bf16),
            pltpu.VMEM((steps, 2 * places, ff), bf16),
            pltpu.VMEM((steps, places, width), bf16),
            pltpu.VMEM((steps, places, width), bf16),
            pltpu.VMEM((steps, rows, width), bf16),
            pltpu.VMEM((steps, rows, width), bf16),
            pltpu.VMEM((2, 2, gu_chunk, 2 * ff), f32),
            pltpu.VMEM((2, gu_chunk, 2 * ff), bf16),
            pltpu.VMEM((2, 2, dn_chunk, dn_cols), f32),
            pltpu.VMEM((2, dn_chunk, dn_cols), bf16),
            dma((4 * steps + 1,)),
            dma((chunks, 3)),
            dma((2 * steps + 1,)),
            dma((2 * steps + 1,)),
            dma((4, steps, half)),
            dma((4, steps, half)),
            dma((chunks, 2 * pairs - 1)),
            dma((chunks, 2 * pairs - 1)),
        ],
        compiler_params=pltpu.CompilerParams(
            collective_id=0, has_side_effects=True, vmem_limit_bytes=63 * 1024 * 1024
        ),
    )(
        tokens, near_tab, far_tab, gate_up_master, gate_up_moment, gate_up_grad,
        down_master, down_moment, down_grad,
    )


def solution(mesh):
    return jax.shard_map(
        per_device,
        mesh=mesh,
        in_specs=(
            P(None, ("engine", "expert"), None),
            P(None, ("engine", "expert"), None),
            P(None, ("engine", "expert"), None),
            P("expert", "engine", None),
            P("expert", "engine", None),
            P("expert", "engine", None),
            P("expert", None, "engine"),
            P("expert", None, "engine"),
            P("expert", None, "engine"),
        ),
        out_specs=P(None, ("engine", "expert"), None),
        check_vma=False,
    )
```

```python
import functools

import jax
import jax.numpy as jnp
from jax import lax
from jax.experimental import pallas as pl
from jax.experimental.pallas import tpu as pltpu
from jax.sharding import PartitionSpec as P

MESH = pl.DeviceIdType.MESH
TILE = 512


def updated(master, moment, grad):
    return (master - 0.5 * (0.8 * moment + 0.2 * grad.astype(jnp.float32))).astype(jnp.bfloat16)


def layer_kernel(
    n_engine,
    n_expert,
    cap,
    tokens,
    near_tab,
    far_tab,
    gu_master,
    gu_moment,
    gu_grad,
    dn_master,
    dn_moment,
    dn_grad,
    mixed,
    gate_up,
    down,
    far_rows,
    relay_tab,
    near_send,
    far_send,
    slots,
    hidden,
    near_back,
    far_back,
    part_recv,
    gu_stage,
    gu_grad_stage,
    dn_stage,
    dn_grad_stage,
    token_sem,
    stage_sem,
    tab_send,
    tab_recv,
    row_send,
    row_recv,
    near_out_send,
    near_out_recv,
    far_out_send,
    far_out_recv,
    near_back_send,
    near_back_recv,
    far_back_send,
    far_back_recv,
    part_send_sem,
    part_recv_sem,
    weight_send,
    weight_recv,
):
    half = n_expert // 2
    lines = half // 2
    pairs = n_engine // 2
    steps, rows, width = mixed.shape
    places = half * cap
    ff = down.shape[0]
    group = width // pairs
    tile = min(TILE, group)
    g, e = lax.axis_index("engine"), lax.axis_index("expert")
    core, pair = lax.rem(g, 2), g // 2
    side, me = e // half, lax.rem(e, half)
    line, inner = lax.rem(me, lines), me // lines
    lands = inner != side
    landing = (g, (1 - side) * half + side * lines + line)
    sibling = (pair * 2 + 1 - core, e)

    def near(j):
        return lax.rem(me + j, half)

    def near_device(index):
        return (g, side * half + index)

    def lander(y):
        return (1 - side) * lines + y

    def source_device(b):
        return (g, (1 - side) * half + b * lines + line)

    def same_core(q):
        return (lax.rem(pair + q, pairs) * 2 + core, e)

    def seats(index, base=0):
        return pl.ds(pl.multiple_of(base + index * cap, 16), cap)

    def columns_of(q):
        start = lax.rem(pair - q + pairs, pairs) * group
        return pl.ds(pl.multiple_of(start, 128), group)

    def tile_of(q, t):
        start = lax.rem(pair - q + pairs, pairs) * group + t * tile
        return pl.ds(pl.multiple_of(start, 128), tile)

    def remote(src, dst, send_sem, recv_sem, device):
        return pltpu.make_async_remote_copy(
            src_ref=src, dst_ref=dst, send_sem=send_sem, recv_sem=recv_sem,
            device_id=device, device_id_type=MESH,
        )

    sends, landing_sends, guarded_sends = [], [], []

    def send(*args):
        copy = remote(*args)
        copy.start()
        sends.append(copy)

    def arrive(dst, sem):
        remote(dst, dst, tab_send.at[0], sem, sibling).wait_recv()

    peers = [landing, (g, (1 - side) * half + (1 - side) * lines + line), sibling]
    peers += [near_device(near(j)) for j in range(1, half)]
    peers += [same_core(q) for q in range(1, pairs)]
    barrier = pltpu.get_barrier_semaphore()
    for device in peers:
        pl.semaphore_signal(barrier, inc=1, device_id=device, device_id_type=MESH)

    pl.semaphore_wait(barrier, len(peers))

    send(far_tab, relay_tab.at[inner], tab_send.at[0], tab_recv.at[inner], landing)
    for s in range(steps):
        send(
            tokens.at[s], far_rows.at[inner, s], row_send.at[s], row_recv.at[inner, s], landing
        )
    own_copy = pltpu.make_async_copy(tokens, mixed, token_sem.at[0])
    own_copy.start()

    gu_rows, dn_cols = gu_master.shape[1], dn_master.shape[2]
    gu_chunk, dn_chunk = gu_stage.shape[2], dn_stage.shape[2]
    n_gu, n_dn = gu_rows // gu_chunk, ff // dn_chunk
    chunks = n_gu + n_dn

    def weight_part(c, owner):
        if c < n_gu:
            start = pl.multiple_of(owner * gu_rows + c * gu_chunk, 16)
            return gate_up.at[pl.ds(start, gu_chunk)]
        columns = pl.ds(pl.multiple_of(owner * dn_cols, 128), dn_cols)
        return down.at[pl.ds((c - n_gu) * dn_chunk, dn_chunk), columns]

    def staged(c):
        slot = c % 2
        if c < n_gu:
            part = pl.ds(c * gu_chunk, gu_chunk)
            refs = (gu_master, gu_moment, gu_grad)
            stages = (gu_stage.at[slot, 0], gu_stage.at[slot, 1], gu_grad_stage.at[slot])
        else:
            part = pl.ds((c - n_gu) * dn_chunk, dn_chunk)
            refs = (dn_master, dn_moment, dn_grad)
            stages = (dn_stage.at[slot, 0], dn_stage.at[slot, 1], dn_grad_stage.at[slot])
        return [
            pltpu.make_async_copy(ref.at[0, part], stage, stage_sem.at[c, i])
            for i, (ref, stage) in enumerate(zip(refs, stages))
        ]

    def prepare(first, last):
        for c in range(first, last):
            if c + 1 < chunks:
                for copy in staged(c + 1):
                    copy.start()
            for copy in staged(c):
                copy.wait()
            slot = c % 2
            mine = weight_part(c, g)
            if c < n_gu:
                mine[...] = updated(gu_stage[slot, 0], gu_stage[slot, 1], gu_grad_stage[slot])
            else:
                mine[...] = updated(dn_stage[slot, 0], dn_stage[slot, 1], dn_grad_stage[slot])
            for q in range(1, pairs):
                send(mine, mine, weight_send.at[c, q], weight_recv.at[c, q], same_core(q))
            send(mine, mine, weight_send.at[c, 0], weight_recv.at[c, 0], sibling)

    def relay(c):
        for q in range(1, pairs):
            owner = lax.rem(pair - q + pairs, pairs) * 2 + core
            part = weight_part(c, owner)
            arrive(part, weight_recv.at[c, q])
            k = pairs + q - 1
            send(part, part, weight_send.at[c, k], weight_recv.at[c, k], sibling)

    def from_sibling(c):
        arrive(weight_part(c, g + 1 - 2 * core), weight_recv.at[c, 0])

    def relayed(c):
        for q in range(1, pairs):
            owner = lax.rem(pair - q + pairs, pairs) * 2 + 1 - core
            arrive(weight_part(c, owner), weight_recv.at[c, pairs + q - 1])

    def select(table, source, outgoing):
        @pl.loop(0, width // TILE)
        def _(t):
            columns = pl.ds(pl.multiple_of(t * TILE, TILE), TILE)
            outgoing[:, columns] = jnp.dot(
                table[...], source[:, columns], preferred_element_type=jnp.float32
            ).astype(jnp.bfloat16)

    def hand_out_near(s):
        select(near_tab.at[s, 0], mixed.at[s], near_send.at[s])
        for j in range(1, half):
            send(
                near_send.at[s, seats(near(j))], slots.at[s, seats(me)],
                near_out_send.at[s, j], near_out_recv.at[s, me], near_device(near(j)),
            )
        pltpu.make_async_copy(
            near_send.at[s, seats(me)], slots.at[s, seats(me)], near_out_recv.at[s, me]
        ).start()

    def far_copies(s, b):
        origin = b * lines + line
        return [
            remote(
                far_send.at[b, s, seats(near(j))], slots.at[s, seats(origin, places)],
                far_out_send.at[b, s, j], far_out_recv.at[s, origin], near_device(near(j)),
            )
            for j in range(1, half)
        ]

    def hand_out_far(s):
        @pl.when(lands)
        def _():
            for b in range(2):
                origin = b * lines + line
                if s == 0:
                    arrive(relay_tab.at[b], tab_recv.at[b])
                arrive(far_rows.at[b, s], row_recv.at[b, s])
                select(relay_tab.at[b, s, 0], far_rows.at[b, s], far_send.at[b, s])
                for copy in far_copies(s, b):
                    copy.start()
                pltpu.make_async_copy(
                    far_send.at[b, s, seats(me)], slots.at[s, seats(origin, places)],
                    far_out_recv.at[s, origin],
                ).start()

        for b in range(2):
            landing_sends.append(functools.partial(far_copies, s, b))

    def project(s):
        for origin in range(half):
            arrive(slots.at[s, seats(origin)], near_out_recv.at[s, origin])
            arrive(slots.at[s, seats(origin, places)], far_out_recv.at[s, origin])

        @pl.loop(0, ff // 256)
        def _(t):
            left = pl.ds(pl.multiple_of(t * 256, 256), 256)
            right = pl.ds(pl.multiple_of(ff + t * 256, 256), 256)
            gate = jnp.dot(slots[s], gate_up[:, left], preferred_element_type=jnp.float32)
            up = jnp.dot(slots[s], gate_up[:, right], preferred_element_type=jnp.float32)
            hidden[:, left] = (gate / (1.0 + jnp.exp(-gate)) * up).astype(jnp.bfloat16)

    def far_return(s, q, y, b):
        columns = columns_of(q)
        return remote(
            slots.at[s, seats(b * lines + y, places), columns],
            far_back.at[b, s, seats(me), columns],
            far_back_send.at[s, q, b, y], far_back_recv.at[b, s, q, me], near_device(lander(y)),
        )

    def expand(s, q):
        @pl.loop(0, group // tile)
        def _(t):
            columns = tile_of(q, t)
            slots[s, :, columns] = jnp.dot(
                hidden[...], down[:, columns], preferred_element_type=jnp.float32
            ).astype(jnp.bfloat16)

        columns = columns_of(q)
        for y in range(lines):
            for b in range(2):
                other = me != lander(y)

                @pl.when(other)
                def _():
                    far_return(s, q, y, b).start()

                @pl.when(jnp.logical_not(other))
                def _():
                    pltpu.make_async_copy(
                        slots.at[s, seats(b * lines + y, places), columns_of(q)],
                        far_back.at[b, s, seats(me), columns_of(q)],
                        far_back_recv.at[b, s, q, me],
                    ).start()

                guarded_sends.append((other, functools.partial(far_return, s, q, y, b)))
        for j in range(1, half):
            send(
                slots.at[s, seats(near(j)), columns], near_back.at[s, seats(me), columns],
                near_back_send.at[s, q, j], near_back_recv.at[s, q, me], near_device(near(j)),
            )
        pltpu.make_async_copy(
            slots.at[s, seats(me), columns], near_back.at[s, seats(me), columns],
            near_back_recv.at[s, q, me],
        ).start()

    def weighted(table, back, columns):
        return lax.dot_general(
            table[...], back[:, columns], (((0,), (0,)), ((), ())),
            preferred_element_type=jnp.float32,
        )

    def part_copy(s, q, b):
        columns = columns_of(q)
        return remote(
            far_rows.at[b, s, :, columns], part_recv.at[s, :, columns],
            part_send_sem.at[b, s, q], part_recv_sem.at[s, q], source_device(b),
        )

    def part_copies(s, q, b):
        return [part_copy(s, q, b)]

    def sum_far(s, q):
        @pl.when(lands)
        def _():
            for b in range(2):
                for origin in range(half):
                    arrive(
                        far_back.at[b, s, seats(origin), columns_of(q)],
                        far_back_recv.at[b, s, q, origin],
                    )

                @pl.loop(0, group // tile)
                def _(t):
                    columns = tile_of(q, t)
                    far_rows[b, s, :, columns] = weighted(
                        relay_tab.at[b, s, 1], far_back.at[b, s], columns
                    ).astype(jnp.bfloat16)

                part_copy(s, q, b).start()

        for b in range(2):
            landing_sends.append(functools.partial(part_copies, s, q, b))

    def finish(s, q):
        for origin in range(half):
            arrive(near_back.at[s, seats(origin), columns_of(q)], near_back_recv.at[s, q, origin])
        arrive(part_recv.at[s, :, columns_of(q)], part_recv_sem.at[s, q])

        @pl.loop(0, group // tile)
        def _(t):
            columns = tile_of(q, t)
            total = weighted(near_tab.at[s, 1], near_back.at[s], columns)
            total = total + part_recv[s, :, columns].astype(jnp.float32)
            mixed[s, :, columns] = total.astype(jnp.bfloat16)

    for copy in staged(0):
        copy.start()
    prepare(0, n_gu // 2)
    own_copy.wait()
    for s in range(steps):
        hand_out_near(s)
    prepare(n_gu // 2, chunks)

    for c in range(n_gu // 2):
        relay(c)
    hand_out_far(0)
    for c in range(n_gu // 2, n_gu):
        relay(c)
    for c in range(n_gu):
        from_sibling(c)
        relayed(c)
    project(0)
    for c in range(n_gu, chunks):
        from_sibling(c)
    expand(0, 0)
    for s in range(1, steps):
        hand_out_far(s)
    for c in range(n_gu, chunks):
        relay(c)
    for c in range(n_gu, chunks):
        relayed(c)
    for q in range(1, pairs):
        expand(0, q)
    sum_far(0, 0)
    for s in range(1, steps):
        project(s)
        for q in range(pairs):
            expand(s, q)
    for s in range(steps):
        for q in range(pairs):
            if (s, q) != (0, 0):
                sum_far(s, q)
    for s in range(steps):
        for q in range(pairs):
            finish(s, q)

    for copy in sends:
        copy.wait_send()
    for other, build in guarded_sends:

        @pl.when(other)
        def _():
            build().wait_send()

    @pl.when(lands)
    def _():
        for build in landing_sends:
            for copy in build():
                copy.wait_send()


def per_device(
    tokens,
    expert_ids,
    route_gain,
    gate_up_master,
    gate_up_moment,
    gate_up_grad,
    down_master,
    down_moment,
    down_grad,
):
    steps, rows, top_k = expert_ids.shape
    width = tokens.shape[2]
    n_engine, n_expert = lax.axis_size("engine"), lax.axis_size("expert")
    half, pairs = n_expert // 2, n_engine // 2
    cap = 3 * rows * top_k // (2 * n_expert)
    cap = -(-cap // 16) * 16
    places = half * cap
    ff = down_master.shape[1]

    named = expert_ids[:, None, :, :] == jnp.arange(n_expert, dtype=jnp.int32)[None, :, None, None]
    share = (route_gain / jnp.sum(route_gain, axis=2, keepdims=True)).astype(jnp.bfloat16)
    chosen = jnp.any(named, axis=3)
    portion = jnp.sum(jnp.where(named, share[:, None].astype(jnp.float32), 0.0), axis=3)
    ahead = jnp.arange(rows)[:, None] < jnp.arange(rows)[None, :]
    place = jnp.einsum(
        "ser,rq->seq", chosen.astype(jnp.bfloat16), ahead.astype(jnp.bfloat16),
        preferred_element_type=jnp.float32,
    ).astype(jnp.int32)
    match = chosen[:, :, None, :] & (
        place[:, :, None, :] == jnp.arange(cap, dtype=jnp.int32)[None, None, :, None]
    )
    table = jnp.stack(
        [match.astype(jnp.bfloat16), jnp.where(match, portion[:, :, None, :], 0.0).astype(jnp.bfloat16)],
        axis=1,
    ).reshape(steps, 2, 2, places, rows)
    side = lax.axis_index("expert") // half
    near_tab = lax.dynamic_index_in_dim(table, side, 2, keepdims=False)
    far_tab = lax.dynamic_index_in_dim(table, 1 - side, 2, keepdims=False)

    gu_rows, dn_cols = gate_up_master.shape[1], down_master.shape[2]
    gu_chunk, dn_chunk = min(128, gu_rows // 4), ff // 8
    chunks = gu_rows // gu_chunk + 8
    lines = half // 2
    bf16, f32 = jnp.bfloat16, jnp.float32
    dma = pltpu.SemaphoreType.DMA
    hbm, vmem = pl.BlockSpec(memory_space=pl.ANY), pl.BlockSpec(memory_space=pltpu.VMEM)
    return pl.pallas_call(
        functools.partial(layer_kernel, n_engine, n_expert, cap),
        out_shape=jax.ShapeDtypeStruct(tokens.shape, bf16),
        in_specs=[hbm, vmem, vmem] + [hbm] * 6,
        out_specs=vmem,
        scratch_shapes=[
            pltpu.VMEM((width, 2 * ff), bf16),
            pltpu.VMEM((ff, width), bf16),
            pltpu.VMEM((2, steps, rows, width), bf16),
            pltpu.VMEM((2, steps, 2, places, rows), bf16),
            pltpu.VMEM((steps, places, width), bf16),
            pltpu.VMEM((2, steps, places, width), bf16),
            pltpu.VMEM((steps, 2 * places, width), bf16),
            pltpu.VMEM((2 * places, ff), bf16),
            pltpu.VMEM((steps, places, width), bf16),
            pltpu.VMEM((2, steps, places, width), bf16),
            pltpu.VMEM((steps, rows, width), bf16),
            pltpu.VMEM((2, 2, gu_chunk, 2 * ff), f32),
            pltpu.VMEM((2, gu_chunk, 2 * ff), bf16),
            pltpu.VMEM((2, 2, dn_chunk, dn_cols), f32),
            pltpu.VMEM((2, dn_chunk, dn_cols), bf16),
            dma((1,)),
            dma((chunks, 3)),
            dma((1,)),
            dma((2,)),
            dma((steps,)),
            dma((2, steps)),
            dma((steps, half)),
            dma((steps, half)),
            dma((2, steps, half)),
            dma((steps, half)),
            dma((steps, pairs, half)),
            dma((steps, pairs, half)),
            dma((steps, pairs, 2, lines)),
            dma((2, steps, pairs, half)),
            dma((2, steps, pairs)),
            dma((steps, pairs)),
            dma((chunks, 2 * pairs - 1)),
            dma((chunks, 2 * pairs - 1)),
        ],
        compiler_params=pltpu.CompilerParams(
            collective_id=0, has_side_effects=True, vmem_limit_bytes=63 * 1024 * 1024
        ),
    )(
        tokens, near_tab, far_tab, gate_up_master, gate_up_moment, gate_up_grad,
        down_master, down_moment, down_grad,
    )


def solution(mesh):
    return jax.shard_map(
        per_device,
        mesh=mesh,
        in_specs=(
            P(None, ("engine", "expert"), None),
            P(None, ("engine", "expert"), None),
            P(None, ("engine", "expert"), None),
            P("expert", "engine", None),
            P("expert", "engine", None),
            P("expert", "engine", None),
            P("expert", None, "engine"),
            P("expert", None, "engine"),
            P("expert", None, "engine"),
        ),
        out_specs=P(None, ("engine", "expert"), None),
        check_vma=False,
    )
```

```python
import functools

import jax
import jax.numpy as jnp
from jax import lax
from jax.experimental import pallas as pl
from jax.experimental.pallas import tpu as pltpu
from jax.sharding import PartitionSpec as P

MESH = pl.DeviceIdType.MESH
TILE = 512


def updated(master, moment, grad):
    return (master - 0.5 * (0.8 * moment + 0.2 * grad.astype(jnp.float32))).astype(jnp.bfloat16)


def layer_kernel(
    n_engine,
    n_expert,
    cap,
    tokens,
    near_tab,
    far_tab,
    gu_master,
    gu_moment,
    gu_grad,
    dn_master,
    dn_moment,
    dn_grad,
    mixed,
    gate_up,
    down,
    far_rows,
    relay_tab,
    near_send,
    far_send,
    slots,
    hidden,
    near_back,
    far_back,
    part_recv,
    gu_stage,
    gu_grad_stage,
    dn_stage,
    dn_grad_stage,
    token_sem,
    stage_sem,
    tab_send,
    tab_recv,
    row_send,
    row_recv,
    near_out_send,
    near_out_recv,
    far_out_send,
    far_out_recv,
    near_back_send,
    near_back_recv,
    far_back_send,
    far_back_recv,
    part_send_sem,
    part_recv_sem,
    weight_send,
    weight_recv,
):
    half = n_expert // 2
    lines = half // 2
    pairs = n_engine // 2
    steps, rows, width = mixed.shape
    places = half * cap
    ff = down.shape[0]
    group = width // pairs
    tile = min(TILE, group)
    g, e = lax.axis_index("engine"), lax.axis_index("expert")
    core, pair = lax.rem(g, 2), g // 2
    side, me = e // half, lax.rem(e, half)
    line, inner = lax.rem(me, lines), me // lines
    lands = inner != side
    landing = (g, (1 - side) * half + side * lines + line)
    sibling = (pair * 2 + 1 - core, e)

    def near(j):
        return lax.rem(me + j, half)

    def near_device(index):
        return (g, side * half + index)

    def lander(y):
        return (1 - side) * lines + y

    def source_device(b):
        return (g, (1 - side) * half + b * lines + line)

    def same_core(q):
        return (lax.rem(pair + q, pairs) * 2 + core, e)

    def seats(index, base=0):
        return pl.ds(pl.multiple_of(base + index * cap, 16), cap)

    def columns_of(q):
        start = lax.rem(pair - q + pairs, pairs) * group
        return pl.ds(pl.multiple_of(start, 128), group)

    def tile_of(q, t):
        start = lax.rem(pair - q + pairs, pairs) * group + t * tile
        return pl.ds(pl.multiple_of(start, 128), tile)

    def remote(src, dst, send_sem, recv_sem, device):
        return pltpu.make_async_remote_copy(
            src_ref=src, dst_ref=dst, send_sem=send_sem, recv_sem=recv_sem,
            device_id=device, device_id_type=MESH,
        )

    sends, landing_sends, guarded_sends = [], [], []

    def send(*args):
        copy = remote(*args)
        copy.start()
        sends.append(copy)

    def arrive(dst, sem):
        remote(dst, dst, tab_send.at[0], sem, sibling).wait_recv()

    peers = [landing, (g, (1 - side) * half + (1 - side) * lines + line), sibling]
    peers += [near_device(near(j)) for j in range(1, half)]
    peers += [same_core(q) for q in range(1, pairs)]
    barrier = pltpu.get_barrier_semaphore()
    for device in peers:
        pl.semaphore_signal(barrier, inc=1, device_id=device, device_id_type=MESH)

    pl.semaphore_wait(barrier, len(peers))

    send(far_tab, relay_tab.at[inner], tab_send.at[0], tab_recv.at[inner], landing)
    pieces = row_send.shape[1]
    piece = rows // pieces

    def send_rows(s, i):
        part = pl.ds(i * piece, piece)
        send(
            tokens.at[s, part], far_rows.at[inner, s, part],
            row_send.at[s, i], row_recv.at[inner, s, i], landing,
        )

    send_rows(0, 0)
    own_copy = pltpu.make_async_copy(tokens, mixed, token_sem.at[0])
    own_copy.start()

    gu_rows, dn_cols = gu_master.shape[1], dn_master.shape[2]
    gu_chunk, dn_chunk = gu_stage.shape[2], dn_stage.shape[2]
    n_gu, n_dn = gu_rows // gu_chunk, ff // dn_chunk
    chunks = n_gu + n_dn

    def weight_part(c, owner):
        if c < n_gu:
            start = pl.multiple_of(owner * gu_rows + c * gu_chunk, 16)
            return gate_up.at[pl.ds(start, gu_chunk)]
        columns = pl.ds(pl.multiple_of(owner * dn_cols, 128), dn_cols)
        return down.at[pl.ds((c - n_gu) * dn_chunk, dn_chunk), columns]

    def staged(c):
        slot = c % 2
        if c < n_gu:
            part = pl.ds(c * gu_chunk, gu_chunk)
            refs = (gu_master, gu_moment, gu_grad)
            stages = (gu_stage.at[slot, 0], gu_stage.at[slot, 1], gu_grad_stage.at[slot])
        else:
            part = pl.ds((c - n_gu) * dn_chunk, dn_chunk)
            refs = (dn_master, dn_moment, dn_grad)
            stages = (dn_stage.at[slot, 0], dn_stage.at[slot, 1], dn_grad_stage.at[slot])
        return [
            pltpu.make_async_copy(ref.at[0, part], stage, stage_sem.at[c, i])
            for i, (ref, stage) in enumerate(zip(refs, stages))
        ]

    def prepare(first, last):
        for c in range(first, last):
            if c + 1 < chunks:
                for copy in staged(c + 1):
                    copy.start()
            for copy in staged(c):
                copy.wait()
            slot = c % 2
            mine = weight_part(c, g)
            if c < n_gu:
                mine[...] = updated(gu_stage[slot, 0], gu_stage[slot, 1], gu_grad_stage[slot])
            else:
                mine[...] = updated(dn_stage[slot, 0], dn_stage[slot, 1], dn_grad_stage[slot])
            for q in range(1, pairs):
                send(mine, mine, weight_send.at[c, q], weight_recv.at[c, q], same_core(q))
            send(mine, mine, weight_send.at[c, 0], weight_recv.at[c, 0], sibling)

    def relay(c):
        for q in range(1, pairs):
            owner = lax.rem(pair - q + pairs, pairs) * 2 + core
            part = weight_part(c, owner)
            arrive(part, weight_recv.at[c, q])
            k = pairs + q - 1
            send(part, part, weight_send.at[c, k], weight_recv.at[c, k], sibling)

    def from_sibling(c):
        arrive(weight_part(c, g + 1 - 2 * core), weight_recv.at[c, 0])

    def relayed(c):
        for q in range(1, pairs):
            owner = lax.rem(pair - q + pairs, pairs) * 2 + 1 - core
            arrive(weight_part(c, owner), weight_recv.at[c, pairs + q - 1])

    def select(table, source, outgoing):
        @pl.loop(0, width // TILE)
        def _(t):
            columns = pl.ds(pl.multiple_of(t * TILE, TILE), TILE)
            outgoing[:, columns] = jnp.dot(
                table[...], source[:, columns], preferred_element_type=jnp.float32
            ).astype(jnp.bfloat16)

    def hand_out_near(s):
        select(near_tab.at[s, 0], mixed.at[s], near_send.at[s])
        for j in range(1, half):
            send(
                near_send.at[s, seats(near(j))], slots.at[s, seats(me)],
                near_out_send.at[s, j], near_out_recv.at[s, me], near_device(near(j)),
            )
        pltpu.make_async_copy(
            near_send.at[s, seats(me)], slots.at[s, seats(me)], near_out_recv.at[s, me]
        ).start()

    def far_copies(s, b):
        origin = b * lines + line
        return [
            remote(
                far_send.at[b, s, seats(near(j))], slots.at[s, seats(origin, places)],
                far_out_send.at[b, s, j], far_out_recv.at[s, origin], near_device(near(j)),
            )
            for j in range(1, half)
        ]

    def hand_out_far(s):
        @pl.when(lands)
        def _():
            for b in range(2):
                origin = b * lines + line
                if s == 0:
                    arrive(relay_tab.at[b], tab_recv.at[b])
                for i in range(pieces):
                    part = pl.ds(i * piece, piece)
                    arrive(far_rows.at[b, s, part], row_recv.at[b, s, i])
                select(relay_tab.at[b, s, 0], far_rows.at[b, s], far_send.at[b, s])
                for copy in far_copies(s, b):
                    copy.start()
                pltpu.make_async_copy(
                    far_send.at[b, s, seats(me)], slots.at[s, seats(origin, places)],
                    far_out_recv.at[s, origin],
                ).start()

        for b in range(2):
            landing_sends.append(functools.partial(far_copies, s, b))

    def project(s):
        for origin in range(half):
            arrive(slots.at[s, seats(origin)], near_out_recv.at[s, origin])
            arrive(slots.at[s, seats(origin, places)], far_out_recv.at[s, origin])

        @pl.loop(0, ff // 256)
        def _(t):
            left = pl.ds(pl.multiple_of(t * 256, 256), 256)
            right = pl.ds(pl.multiple_of(ff + t * 256, 256), 256)
            gate = jnp.dot(slots[s], gate_up[:, left], preferred_element_type=jnp.float32)
            up = jnp.dot(slots[s], gate_up[:, right], preferred_element_type=jnp.float32)
            hidden[:, left] = (gate / (1.0 + jnp.exp(-gate)) * up).astype(jnp.bfloat16)

    def far_return(s, q, y, b):
        columns = columns_of(q)
        return remote(
            slots.at[s, seats(b * lines + y, places), columns],
            far_back.at[b, s, seats(me), columns],
            far_back_send.at[s, q, b, y], far_back_recv.at[b, s, q, me], near_device(lander(y)),
        )

    def expand(s, q):
        @pl.loop(0, group // tile)
        def _(t):
            columns = tile_of(q, t)
            slots[s, :, columns] = jnp.dot(
                hidden[...], down[:, columns], preferred_element_type=jnp.float32
            ).astype(jnp.bfloat16)

        columns = columns_of(q)
        for y in range(lines):
            for b in range(2):
                other = me != lander(y)

                @pl.when(other)
                def _():
                    far_return(s, q, y, b).start()

                @pl.when(jnp.logical_not(other))
                def _():
                    pltpu.make_async_copy(
                        slots.at[s, seats(b * lines + y, places), columns_of(q)],
                        far_back.at[b, s, seats(me), columns_of(q)],
                        far_back_recv.at[b, s, q, me],
                    ).start()

                guarded_sends.append((other, functools.partial(far_return, s, q, y, b)))
        for j in range(1, half):
            send(
                slots.at[s, seats(near(j)), columns], near_back.at[s, seats(me), columns],
                near_back_send.at[s, q, j], near_back_recv.at[s, q, me], near_device(near(j)),
            )
        pltpu.make_async_copy(
            slots.at[s, seats(me), columns], near_back.at[s, seats(me), columns],
            near_back_recv.at[s, q, me],
        ).start()

    def weighted(table, back, columns):
        return lax.dot_general(
            table[...], back[:, columns], (((0,), (0,)), ((), ())),
            preferred_element_type=jnp.float32,
        )

    def part_copy(s, q, b):
        columns = columns_of(q)
        return remote(
            far_rows.at[b, s, :, columns], part_recv.at[s, :, columns],
            part_send_sem.at[b, s, q], part_recv_sem.at[s, q], source_device(b),
        )

    def part_copies(s, q, b):
        return [part_copy(s, q, b)]

    def sum_far(s, q):
        @pl.when(lands)
        def _():
            for b in range(2):
                for origin in range(half):
                    arrive(
                        far_back.at[b, s, seats(origin), columns_of(q)],
                        far_back_recv.at[b, s, q, origin],
                    )

                @pl.loop(0, group // tile)
                def _(t):
                    columns = tile_of(q, t)
                    far_rows[b, s, :, columns] = weighted(
                        relay_tab.at[b, s, 1], far_back.at[b, s], columns
                    ).astype(jnp.bfloat16)

                part_copy(s, q, b).start()

        for b in range(2):
            landing_sends.append(functools.partial(part_copies, s, q, b))

    def finish(s, q):
        for origin in range(half):
            arrive(near_back.at[s, seats(origin), columns_of(q)], near_back_recv.at[s, q, origin])
        arrive(part_recv.at[s, :, columns_of(q)], part_recv_sem.at[s, q])

        @pl.loop(0, group // tile)
        def _(t):
            columns = tile_of(q, t)
            total = weighted(near_tab.at[s, 1], near_back.at[s], columns)
            total = total + part_recv[s, :, columns].astype(jnp.float32)
            mixed[s, :, columns] = total.astype(jnp.bfloat16)

    for copy in staged(0):
        copy.start()
    pending = [(s, i) for s in range(steps) for i in range(pieces)][1:]
    done = 0
    for s in range(steps):
        upto = (s + 1) * n_gu // steps
        while done < upto:
            prepare(done, done + 1)
            done += 1
            if pending:
                send_rows(*pending.pop(0))
        if s == 0:
            own_copy.wait()
        hand_out_near(s)
    while pending:
        send_rows(*pending.pop(0))
    prepare(n_gu, chunks)

    for c in range(n_gu // 2):
        relay(c)
    hand_out_far(0)
    for c in range(n_gu // 2, n_gu):
        relay(c)
    for c in range(n_gu):
        from_sibling(c)
        relayed(c)
    project(0)
    for c in range(n_gu, chunks):
        from_sibling(c)
    expand(0, 0)
    for s in range(1, steps):
        hand_out_far(s)
    for c in range(n_gu, chunks):
        relay(c)
    for c in range(n_gu, chunks):
        relayed(c)
    for q in range(1, pairs):
        expand(0, q)
    sum_far(0, 0)
    for s in range(1, steps):
        project(s)
        for q in range(pairs):
            expand(s, q)
    for s in range(steps):
        for q in range(pairs):
            if (s, q) != (0, 0):
                sum_far(s, q)
    for s in range(steps):
        for q in range(pairs):
            finish(s, q)

    for copy in sends:
        copy.wait_send()
    for other, build in guarded_sends:

        @pl.when(other)
        def _():
            build().wait_send()

    @pl.when(lands)
    def _():
        for build in landing_sends:
            for copy in build():
                copy.wait_send()


def per_device(
    tokens,
    expert_ids,
    route_gain,
    gate_up_master,
    gate_up_moment,
    gate_up_grad,
    down_master,
    down_moment,
    down_grad,
):
    steps, rows, top_k = expert_ids.shape
    width = tokens.shape[2]
    n_engine, n_expert = lax.axis_size("engine"), lax.axis_size("expert")
    half, pairs = n_expert // 2, n_engine // 2
    cap = 3 * rows * top_k // (2 * n_expert)
    cap = -(-cap // 16) * 16
    places = half * cap
    ff = down_master.shape[1]

    named = expert_ids[:, None, :, :] == jnp.arange(n_expert, dtype=jnp.int32)[None, :, None, None]
    share = (route_gain / jnp.sum(route_gain, axis=2, keepdims=True)).astype(jnp.bfloat16)
    chosen = jnp.any(named, axis=3)
    portion = jnp.sum(jnp.where(named, share[:, None].astype(jnp.float32), 0.0), axis=3)
    ahead = jnp.arange(rows)[:, None] < jnp.arange(rows)[None, :]
    place = jnp.einsum(
        "ser,rq->seq", chosen.astype(jnp.bfloat16), ahead.astype(jnp.bfloat16),
        preferred_element_type=jnp.float32,
    ).astype(jnp.int32)
    match = chosen[:, :, None, :] & (
        place[:, :, None, :] == jnp.arange(cap, dtype=jnp.int32)[None, None, :, None]
    )
    table = jnp.stack(
        [match.astype(jnp.bfloat16), jnp.where(match, portion[:, :, None, :], 0.0).astype(jnp.bfloat16)],
        axis=1,
    ).reshape(steps, 2, 2, places, rows)
    side = lax.axis_index("expert") // half
    near_tab = lax.dynamic_index_in_dim(table, side, 2, keepdims=False)
    far_tab = lax.dynamic_index_in_dim(table, 1 - side, 2, keepdims=False)

    gu_rows, dn_cols = gate_up_master.shape[1], down_master.shape[2]
    gu_chunk, dn_chunk = min(128, gu_rows // 4), ff // 4
    chunks = gu_rows // gu_chunk + 4
    lines = half // 2
    bf16, f32 = jnp.bfloat16, jnp.float32
    dma = pltpu.SemaphoreType.DMA
    hbm, vmem = pl.BlockSpec(memory_space=pl.ANY), pl.BlockSpec(memory_space=pltpu.VMEM)
    return pl.pallas_call(
        functools.partial(layer_kernel, n_engine, n_expert, cap),
        out_shape=jax.ShapeDtypeStruct(tokens.shape, bf16),
        in_specs=[hbm, vmem, vmem] + [hbm] * 6,
        out_specs=vmem,
        scratch_shapes=[
            pltpu.VMEM((width, 2 * ff), bf16),
            pltpu.VMEM((ff, width), bf16),
            pltpu.VMEM((2, steps, rows, width), bf16),
            pltpu.VMEM((2, steps, 2, places, rows), bf16),
            pltpu.VMEM((steps, places, width), bf16),
            pltpu.VMEM((2, steps, places, width), bf16),
            pltpu.VMEM((steps, 2 * places, width), bf16),
            pltpu.VMEM((2 * places, ff), bf16),
            pltpu.VMEM((steps, places, width), bf16),
            pltpu.VMEM((2, steps, places, width), bf16),
            pltpu.VMEM((steps, rows, width), bf16),
            pltpu.VMEM((2, 2, gu_chunk, 2 * ff), f32),
            pltpu.VMEM((2, gu_chunk, 2 * ff), bf16),
            pltpu.VMEM((2, 2, dn_chunk, dn_cols), f32),
            pltpu.VMEM((2, dn_chunk, dn_cols), bf16),
            dma((1,)),
            dma((chunks, 3)),
            dma((1,)),
            dma((2,)),
            dma((steps, 4)),
            dma((2, steps, 4)),
            dma((steps, half)),
            dma((steps, half)),
            dma((2, steps, half)),
            dma((steps, half)),
            dma((steps, pairs, half)),
            dma((steps, pairs, half)),
            dma((steps, pairs, 2, lines)),
            dma((2, steps, pairs, half)),
            dma((2, steps, pairs)),
            dma((steps, pairs)),
            dma((chunks, 2 * pairs - 1)),
            dma((chunks, 2 * pairs - 1)),
        ],
        compiler_params=pltpu.CompilerParams(
            collective_id=0, has_side_effects=True, vmem_limit_bytes=63 * 1024 * 1024
        ),
    )(
        tokens, near_tab, far_tab, gate_up_master, gate_up_moment, gate_up_grad,
        down_master, down_moment, down_grad,
    )


def solution(mesh):
    return jax.shard_map(
        per_device,
        mesh=mesh,
        in_specs=(
            P(None, ("engine", "expert"), None),
            P(None, ("engine", "expert"), None),
            P(None, ("engine", "expert"), None),
            P("expert", "engine", None),
            P("expert", "engine", None),
            P("expert", "engine", None),
            P("expert", None, "engine"),
            P("expert", None, "engine"),
            P("expert", None, "engine"),
        ),
        out_specs=P(None, ("engine", "expert"), None),
        check_vma=False,
    )
```

```python
import functools

import jax
import jax.numpy as jnp
from jax import lax
from jax.experimental import pallas as pl
from jax.experimental.pallas import tpu as pltpu
from jax.sharding import PartitionSpec as P

MESH = pl.DeviceIdType.MESH
TILE = 512


def updated(master, moment, grad):
    return (master - 0.5 * (0.8 * moment + 0.2 * grad.astype(jnp.float32))).astype(jnp.bfloat16)


def layer_kernel(
    n_engine,
    n_expert,
    cap,
    tokens,
    near_tab,
    far_tab,
    gu_master,
    gu_moment,
    gu_grad,
    dn_master,
    dn_moment,
    dn_grad,
    mixed,
    gate_up,
    down,
    far_rows,
    relay_tab,
    near_send,
    far_send,
    slots,
    hidden,
    near_back,
    far_back,
    part_recv,
    gu_stage,
    gu_grad_stage,
    dn_stage,
    dn_grad_stage,
    token_sem,
    stage_sem,
    tab_send,
    tab_recv,
    row_send,
    row_recv,
    near_out_send,
    near_out_recv,
    far_out_send,
    far_out_recv,
    near_back_send,
    near_back_recv,
    far_back_send,
    far_back_recv,
    part_send_sem,
    part_recv_sem,
    weight_send,
    weight_recv,
):
    half = n_expert // 2
    lines = half // 2
    pairs = n_engine // 2
    steps, rows, width = mixed.shape
    places = half * cap
    ff = down.shape[0]
    group = width // pairs
    tile = min(TILE, group)
    g, e = lax.axis_index("engine"), lax.axis_index("expert")
    core, pair = lax.rem(g, 2), g // 2
    side, me = e // half, lax.rem(e, half)
    line, inner = lax.rem(me, lines), me // lines
    lands = inner != side
    landing = (g, (1 - side) * half + side * lines + line)
    sibling = (pair * 2 + 1 - core, e)

    def near(j):
        return lax.rem(me + j, half)

    def near_device(index):
        return (g, side * half + index)

    def lander(y):
        return (1 - side) * lines + y

    def source_device(b):
        return (g, (1 - side) * half + b * lines + line)

    def same_core(q):
        return (lax.rem(pair + q, pairs) * 2 + core, e)

    def seats(index, base=0):
        return pl.ds(pl.multiple_of(base + index * cap, 16), cap)

    def columns_of(q):
        start = lax.rem(pair - q + pairs, pairs) * group
        return pl.ds(pl.multiple_of(start, 128), group)

    def tile_of(q, t):
        start = lax.rem(pair - q + pairs, pairs) * group + t * tile
        return pl.ds(pl.multiple_of(start, 128), tile)

    def remote(src, dst, send_sem, recv_sem, device):
        return pltpu.make_async_remote_copy(
            src_ref=src, dst_ref=dst, send_sem=send_sem, recv_sem=recv_sem,
            device_id=device, device_id_type=MESH,
        )

    sends, landing_sends, guarded_sends = [], [], []

    def send(*args):
        copy = remote(*args)
        copy.start()
        sends.append(copy)

    def arrive(dst, sem):
        remote(dst, dst, tab_send.at[0], sem, sibling).wait_recv()

    peers = [landing, (g, (1 - side) * half + (1 - side) * lines + line), sibling]
    peers += [near_device(near(j)) for j in range(1, half)]
    peers += [same_core(q) for q in range(1, pairs)]
    barrier = pltpu.get_barrier_semaphore()
    for device in peers:
        pl.semaphore_signal(barrier, inc=1, device_id=device, device_id_type=MESH)

    pl.semaphore_wait(barrier, len(peers))

    send(far_tab, relay_tab.at[inner], tab_send.at[0], tab_recv.at[inner], landing)
    pieces = row_send.shape[1]
    piece = rows // pieces

    def send_rows(s, i):
        part = pl.ds(i * piece, piece)
        send(
            tokens.at[s, part], far_rows.at[inner, s, part],
            row_send.at[s, i], row_recv.at[inner, s, i], landing,
        )

    send_rows(0, 0)
    own_copy = pltpu.make_async_copy(tokens, mixed, token_sem.at[0])
    own_copy.start()

    gu_rows, dn_cols = gu_master.shape[1], dn_master.shape[2]
    gu_chunk, dn_chunk = gu_stage.shape[2], dn_stage.shape[2]
    n_gu, n_dn = gu_rows // gu_chunk, ff // dn_chunk
    chunks = n_gu + n_dn

    def weight_part(c, owner):
        if c < n_gu:
            start = pl.multiple_of(owner * gu_rows + c * gu_chunk, 16)
            return gate_up.at[pl.ds(start, gu_chunk)]
        columns = pl.ds(pl.multiple_of(owner * dn_cols, 128), dn_cols)
        return down.at[pl.ds((c - n_gu) * dn_chunk, dn_chunk), columns]

    def staged(c):
        slot = c % 2
        if c < n_gu:
            part = pl.ds(c * gu_chunk, gu_chunk)
            refs = (gu_master, gu_moment, gu_grad)
            stages = (gu_stage.at[slot, 0], gu_stage.at[slot, 1], gu_grad_stage.at[slot])
        else:
            part = pl.ds((c - n_gu) * dn_chunk, dn_chunk)
            refs = (dn_master, dn_moment, dn_grad)
            stages = (dn_stage.at[slot, 0], dn_stage.at[slot, 1], dn_grad_stage.at[slot])
        return [
            pltpu.make_async_copy(ref.at[0, part], stage, stage_sem.at[c, i])
            for i, (ref, stage) in enumerate(zip(refs, stages))
        ]

    def prepare(first, last):
        for c in range(first, last):
            if c + 1 < chunks:
                for copy in staged(c + 1):
                    copy.start()
            for copy in staged(c):
                copy.wait()
            slot = c % 2
            mine = weight_part(c, g)
            if c < n_gu:
                mine[...] = updated(gu_stage[slot, 0], gu_stage[slot, 1], gu_grad_stage[slot])
            else:
                mine[...] = updated(dn_stage[slot, 0], dn_stage[slot, 1], dn_grad_stage[slot])
            for q in range(1, pairs):
                send(mine, mine, weight_send.at[c, q], weight_recv.at[c, q], same_core(q))
            send(mine, mine, weight_send.at[c, 0], weight_recv.at[c, 0], sibling)

    def relay(c):
        for q in range(1, pairs):
            owner = lax.rem(pair - q + pairs, pairs) * 2 + core
            part = weight_part(c, owner)
            arrive(part, weight_recv.at[c, q])
            k = pairs + q - 1
            send(part, part, weight_send.at[c, k], weight_recv.at[c, k], sibling)

    def from_sibling(c):
        arrive(weight_part(c, g + 1 - 2 * core), weight_recv.at[c, 0])

    def relayed(c):
        for q in range(1, pairs):
            owner = lax.rem(pair - q + pairs, pairs) * 2 + 1 - core
            arrive(weight_part(c, owner), weight_recv.at[c, pairs + q - 1])

    def select(table, source, outgoing):
        @pl.loop(0, width // TILE)
        def _(t):
            columns = pl.ds(pl.multiple_of(t * TILE, TILE), TILE)
            outgoing[:, columns] = jnp.dot(
                table[...], source[:, columns], preferred_element_type=jnp.float32
            ).astype(jnp.bfloat16)

    def hand_out_near(s):
        select(near_tab.at[s, 0], mixed.at[s], near_send.at[s])
        for j in range(1, half):
            send(
                near_send.at[s, seats(near(j))], slots.at[s, seats(me)],
                near_out_send.at[s, j], near_out_recv.at[s, me], near_device(near(j)),
            )
        pltpu.make_async_copy(
            near_send.at[s, seats(me)], slots.at[s, seats(me)], near_out_recv.at[s, me]
        ).start()

    def far_copies(s, b):
        origin = b * lines + line
        return [
            remote(
                far_send.at[b, s, seats(near(j))], slots.at[s, seats(origin, places)],
                far_out_send.at[b, s, j], far_out_recv.at[s, origin], near_device(near(j)),
            )
            for j in range(1, half)
        ]

    def hand_out_far(s):
        @pl.when(lands)
        def _():
            for b in range(2):
                origin = b * lines + line
                if s == 0:
                    arrive(relay_tab.at[b], tab_recv.at[b])
                for i in range(pieces):
                    part = pl.ds(i * piece, piece)
                    arrive(far_rows.at[b, s, part], row_recv.at[b, s, i])
                select(relay_tab.at[b, s, 0], far_rows.at[b, s], far_send.at[b, s])
                for copy in far_copies(s, b):
                    copy.start()
                pltpu.make_async_copy(
                    far_send.at[b, s, seats(me)], slots.at[s, seats(origin, places)],
                    far_out_recv.at[s, origin],
                ).start()

        for b in range(2):
            landing_sends.append(functools.partial(far_copies, s, b))

    def project(s):
        for origin in range(half):
            arrive(slots.at[s, seats(origin)], near_out_recv.at[s, origin])
            arrive(slots.at[s, seats(origin, places)], far_out_recv.at[s, origin])

        @pl.loop(0, ff // 256)
        def _(t):
            left = pl.ds(pl.multiple_of(t * 256, 256), 256)
            right = pl.ds(pl.multiple_of(ff + t * 256, 256), 256)
            gate = jnp.dot(slots[s], gate_up[:, left], preferred_element_type=jnp.float32)
            up = jnp.dot(slots[s], gate_up[:, right], preferred_element_type=jnp.float32)
            hidden[:, left] = (gate / (1.0 + jnp.exp(-gate)) * up).astype(jnp.bfloat16)

    def far_return(s, q, y, b):
        columns = columns_of(q)
        return remote(
            slots.at[s, seats(b * lines + y, places), columns],
            far_back.at[b, s, seats(me), columns],
            far_back_send.at[s, q, b, y], far_back_recv.at[b, s, q, me], near_device(lander(y)),
        )

    def expand(s, q):
        @pl.loop(0, group // tile)
        def _(t):
            columns = tile_of(q, t)
            slots[s, :, columns] = jnp.dot(
                hidden[...], down[:, columns], preferred_element_type=jnp.float32
            ).astype(jnp.bfloat16)

        columns = columns_of(q)
        for y in range(lines):
            for b in range(2):
                other = me != lander(y)

                @pl.when(other)
                def _():
                    far_return(s, q, y, b).start()

                @pl.when(jnp.logical_not(other))
                def _():
                    pltpu.make_async_copy(
                        slots.at[s, seats(b * lines + y, places), columns_of(q)],
                        far_back.at[b, s, seats(me), columns_of(q)],
                        far_back_recv.at[b, s, q, me],
                    ).start()

                guarded_sends.append((other, functools.partial(far_return, s, q, y, b)))
        for j in range(1, half):
            send(
                slots.at[s, seats(near(j)), columns], near_back.at[s, seats(me), columns],
                near_back_send.at[s, q, j], near_back_recv.at[s, q, me], near_device(near(j)),
            )
        pltpu.make_async_copy(
            slots.at[s, seats(me), columns], near_back.at[s, seats(me), columns],
            near_back_recv.at[s, q, me],
        ).start()

    def weighted(table, back, columns):
        return lax.dot_general(
            table[...], back[:, columns], (((0,), (0,)), ((), ())),
            preferred_element_type=jnp.float32,
        )

    def part_copy(s, q, b):
        columns = columns_of(q)
        return remote(
            far_rows.at[b, s, :, columns], part_recv.at[s, :, columns],
            part_send_sem.at[b, s, q], part_recv_sem.at[s, q], source_device(b),
        )

    def part_copies(s, q, b):
        return [part_copy(s, q, b)]

    def sum_far(s, q):
        @pl.when(lands)
        def _():
            for b in range(2):
                for origin in range(half):
                    arrive(
                        far_back.at[b, s, seats(origin), columns_of(q)],
                        far_back_recv.at[b, s, q, origin],
                    )

                @pl.loop(0, group // tile)
                def _(t):
                    columns = tile_of(q, t)
                    far_rows[b, s, :, columns] = weighted(
                        relay_tab.at[b, s, 1], far_back.at[b, s], columns
                    ).astype(jnp.bfloat16)

                part_copy(s, q, b).start()

        for b in range(2):
            landing_sends.append(functools.partial(part_copies, s, q, b))

    def finish(s, q):
        for origin in range(half):
            arrive(near_back.at[s, seats(origin), columns_of(q)], near_back_recv.at[s, q, origin])
        arrive(part_recv.at[s, :, columns_of(q)], part_recv_sem.at[s, q])

        @pl.loop(0, group // tile)
        def _(t):
            columns = tile_of(q, t)
            total = weighted(near_tab.at[s, 1], near_back.at[s], columns)
            total = total + part_recv[s, :, columns].astype(jnp.float32)
            mixed[s, :, columns] = total.astype(jnp.bfloat16)

    for copy in staged(0):
        copy.start()
    pending = [(s, i) for s in range(steps) for i in range(pieces)][1:]
    done = 0
    for s in range(steps):
        upto = (s + 1) * n_gu // steps
        while done < upto:
            prepare(done, done + 1)
            done += 1
            if pending:
                send_rows(*pending.pop(0))
        if s == 0:
            own_copy.wait()
        hand_out_near(s)
    while pending:
        send_rows(*pending.pop(0))
    prepare(n_gu, chunks)

    for c in range(n_gu // 2):
        relay(c)
    hand_out_far(0)
    for c in range(n_gu // 2, n_gu):
        relay(c)
    for s in range(1, steps):
        hand_out_far(s)
    for c in range(n_gu):
        from_sibling(c)
        relayed(c)
    project(0)
    for c in range(n_gu, chunks):
        from_sibling(c)
    expand(0, 0)
    for c in range(n_gu, chunks):
        relay(c)
    for c in range(n_gu, chunks):
        relayed(c)
    for q in range(1, pairs):
        expand(0, q)
    sum_far(0, 0)
    for s in range(1, steps):
        project(s)
        for q in range(pairs):
            expand(s, q)
    for s in range(steps):
        for q in range(pairs):
            if (s, q) != (0, 0):
                sum_far(s, q)
    for s in range(steps):
        for q in range(pairs):
            finish(s, q)

    for copy in sends:
        copy.wait_send()
    for other, build in guarded_sends:

        @pl.when(other)
        def _():
            build().wait_send()

    @pl.when(lands)
    def _():
        for build in landing_sends:
            for copy in build():
                copy.wait_send()


def per_device(
    tokens,
    expert_ids,
    route_gain,
    gate_up_master,
    gate_up_moment,
    gate_up_grad,
    down_master,
    down_moment,
    down_grad,
):
    steps, rows, top_k = expert_ids.shape
    width = tokens.shape[2]
    n_engine, n_expert = lax.axis_size("engine"), lax.axis_size("expert")
    half, pairs = n_expert // 2, n_engine // 2
    cap = 3 * rows * top_k // (2 * n_expert)
    cap = -(-cap // 16) * 16
    places = half * cap
    ff = down_master.shape[1]

    named = expert_ids[:, None, :, :] == jnp.arange(n_expert, dtype=jnp.int32)[None, :, None, None]
    share = (route_gain / jnp.sum(route_gain, axis=2, keepdims=True)).astype(jnp.bfloat16)
    chosen = jnp.any(named, axis=3)
    portion = jnp.sum(jnp.where(named, share[:, None].astype(jnp.float32), 0.0), axis=3)
    ahead = jnp.arange(rows)[:, None] < jnp.arange(rows)[None, :]
    place = jnp.einsum(
        "ser,rq->seq", chosen.astype(jnp.bfloat16), ahead.astype(jnp.bfloat16),
        preferred_element_type=jnp.float32,
    ).astype(jnp.int32)
    match = chosen[:, :, None, :] & (
        place[:, :, None, :] == jnp.arange(cap, dtype=jnp.int32)[None, None, :, None]
    )
    table = jnp.stack(
        [match.astype(jnp.bfloat16), jnp.where(match, portion[:, :, None, :], 0.0).astype(jnp.bfloat16)],
        axis=1,
    ).reshape(steps, 2, 2, places, rows)
    side = lax.axis_index("expert") // half
    near_tab = lax.dynamic_index_in_dim(table, side, 2, keepdims=False)
    far_tab = lax.dynamic_index_in_dim(table, 1 - side, 2, keepdims=False)

    gu_rows, dn_cols = gate_up_master.shape[1], down_master.shape[2]
    gu_chunk, dn_chunk = min(128, gu_rows // 4), ff // 4
    chunks = gu_rows // gu_chunk + 4
    lines = half // 2
    bf16, f32 = jnp.bfloat16, jnp.float32
    dma = pltpu.SemaphoreType.DMA
    hbm, vmem = pl.BlockSpec(memory_space=pl.ANY), pl.BlockSpec(memory_space=pltpu.VMEM)
    return pl.pallas_call(
        functools.partial(layer_kernel, n_engine, n_expert, cap),
        out_shape=jax.ShapeDtypeStruct(tokens.shape, bf16),
        in_specs=[hbm, vmem, vmem] + [hbm] * 6,
        out_specs=vmem,
        scratch_shapes=[
            pltpu.VMEM((width, 2 * ff), bf16),
            pltpu.VMEM((ff, width), bf16),
            pltpu.VMEM((2, steps, rows, width), bf16),
            pltpu.VMEM((2, steps, 2, places, rows), bf16),
            pltpu.VMEM((steps, places, width), bf16),
            pltpu.VMEM((2, steps, places, width), bf16),
            pltpu.VMEM((steps, 2 * places, width), bf16),
            pltpu.VMEM((2 * places, ff), bf16),
            pltpu.VMEM((steps, places, width), bf16),
            pltpu.VMEM((2, steps, places, width), bf16),
            pltpu.VMEM((steps, rows, width), bf16),
            pltpu.VMEM((2, 2, gu_chunk, 2 * ff), f32),
            pltpu.VMEM((2, gu_chunk, 2 * ff), bf16),
            pltpu.VMEM((2, 2, dn_chunk, dn_cols), f32),
            pltpu.VMEM((2, dn_chunk, dn_cols), bf16),
            dma((1,)),
            dma((chunks, 3)),
            dma((1,)),
            dma((2,)),
            dma((steps, 4)),
            dma((2, steps, 4)),
            dma((steps, half)),
            dma((steps, half)),
            dma((2, steps, half)),
            dma((steps, half)),
            dma((steps, pairs, half)),
            dma((steps, pairs, half)),
            dma((steps, pairs, 2, lines)),
            dma((2, steps, pairs, half)),
            dma((2, steps, pairs)),
            dma((steps, pairs)),
            dma((chunks, 2 * pairs - 1)),
            dma((chunks, 2 * pairs - 1)),
        ],
        compiler_params=pltpu.CompilerParams(
            collective_id=0, has_side_effects=True, vmem_limit_bytes=63 * 1024 * 1024
        ),
    )(
        tokens, near_tab, far_tab, gate_up_master, gate_up_moment, gate_up_grad,
        down_master, down_moment, down_grad,
    )


def solution(mesh):
    return jax.shard_map(
        per_device,
        mesh=mesh,
        in_specs=(
            P(None, ("engine", "expert"), None),
            P(None, ("engine", "expert"), None),
            P(None, ("engine", "expert"), None),
            P("expert", "engine", None),
            P("expert", "engine", None),
            P("expert", "engine", None),
            P("expert", None, "engine"),
            P("expert", None, "engine"),
            P("expert", None, "engine"),
        ),
        out_specs=P(None, ("engine", "expert"), None),
        check_vma=False,
    )
```
